512 devices in a mesh: task: 128 (over z, y, core), aux: 4 (over x).
Axes of the slice: x: 4, y: 8, z: 8, core: 2. Of those that a mesh axis runs over, the one named last changes fastest.
Arguments:
- factors: bfloat16 [128, 2048, 1024], P('task', 'aux'), may hold values from -0.125 to 0.125
- amplitudes: bfloat16 [128, 256, 1024], P('task'), may hold values from -6 to 6
- task_counts: int32 [128], P('task'), may hold values from 1 to 4, 256 in all
- task_tiles: int32 [128, 4, 3], P('task'), may hold values from 0 to 4
Outputs:
- residual: float32 [128, 256, 1024], P('task', None, 'aux')
The draws below stay inside these ranges and needn't reach their ends.
Inputs may be any that keep to these rules, and one draw needn't show every extreme that they name: `task_counts`: every tile has 1 to 4 tasks, exactly 256 in all; some tile has exactly 4.
All inputs are finite; a program needn't handle non-finite values. No bound on the sum of `task_counts` on one device may be relied on, other than what follows from the above.
Results may differ from the reference program's by a relative error of at most 0.0026.
Values may be sent and summed in bfloat16 or wider, within the bound.
No kernel may reach another device: no remote copies, remote signals or barrier semaphores. Data moves between devices by JAX's collectives and lax.ppermute only.
A program may use at most 64 MiB of HBM per device.

```python
import math
import jax
import jax.numpy as jnp
import numpy as np
from jax import lax

AUX = 2048
VB = 32
PAIRS = 1024
OCCP = 256
MOST = 4
RADIUS = 2
TILES = 128
TASKS = 256
N_AUX = 4


def place_ends(result, stream_key, smallest, top_value):
    index_at = [jax.random.randint(jax.random.fold_in(stream_key, axis), (), 0, length) for axis, length in enumerate(result.shape)]
    widest = result.shape.index(max(result.shape))
    neighbour = index_at[:widest] + [(index_at[widest] + 1) % result.shape[widest]] + index_at[widest + 1:]
    return result.at[tuple(index_at)].set(smallest).at[tuple(neighbour)].set(top_value)


def steps_of(key, dims, cuts, smallest, top_value):
    gain, own = 1.0, jax.random.fold_in(key, 6)
    for position, shards_of in cuts:
        steps = jnp.exp(jax.random.uniform(jax.random.fold_in(own, position), (shards_of,), jnp.float32, smallest / len(cuts), top_value / len(cuts)))
        gain = gain * jnp.repeat(steps, dims[position] // shards_of).reshape([-1 if axis == position else 1 for axis in range(len(dims))])
    return gain


def profile(count, total, bound, slope):
    weights = [(1 << 20) // math.isqrt(grade ** slope) + 1 for grade in range(2, count + 1)]
    rest, counts = total - bound - (count - 1), [1] * (count - 1)
    while rest > 0:
        movable = [i for i in range(count - 1) if counts[i] < bound]
        pool, remaining = sum([weights[i] for i in movable]), rest
        for i in movable:
            addition = min(bound - counts[i], max(1, remaining * weights[i] // pool), rest)
            counts[i] = counts[i] + addition
            rest = rest - addition
    return np.array([bound] + counts)


def uneven(stream_key, amount, total, bound, skew):
    if amount == 2:
        one = jax.random.randint(stream_key, (), max(1, total - bound), min(bound, total - 1) + 1)
        return jnp.stack([one, total - one])
    tallies = jnp.asarray(profile(amount, total, bound, skew), jnp.int32)
    pairs = (amount - 1) // 2
    giver, sink = tallies[1:1 + 2 * pairs:2], tallies[2:2 + 2 * pairs:2]
    margin = jnp.minimum(giver - 1, bound - sink)
    moved = jax.random.randint(jax.random.fold_in(stream_key, 1), (pairs,), 0, 1 << 20) % (margin + 1)
    tallies = tallies.at[1:1 + 2 * pairs:2].set(giver - moved).at[2:2 + 2 * pairs:2].set(sink + moved)
    return tallies[jax.random.permutation(jax.random.fold_in(stream_key, 2), amount)]


def gaussian(own_key, dims, spread, reach, shards=(), kind=jnp.bfloat16):
    result = jax.random.normal(own_key, dims, jnp.float32) * spread
    if len(shards) > 0:
        result = steps_of(own_key, dims, shards, -0.22, 0.18) * result
    return jnp.clip(result, min=-reach, max=reach).astype(kind)


def setup_inputs(seed: int = 0) -> dict:
    seeds = jax.random.split(jax.random.key(seed), 5)
    return {
        "factors": gaussian(seeds[0], (TILES, AUX, PAIRS), AUX ** -0.5, 0.125, ((0, 128), (1, 4))),
        "amplitudes": gaussian(seeds[1], (TILES, OCCP, PAIRS), 1.0, 6.0, ((0, 128),)),
        "task_counts": uneven(seeds[2], TILES, TASKS, MOST, 2).astype(jnp.int32),
        "task_tiles": place_ends(jax.random.randint(seeds[3], (TILES, MOST, 3), 0, 2 * RADIUS + 1), jax.random.fold_in(seeds[3], 1), 0, 2 * RADIUS).astype(jnp.int32),
    }


def quarter_term(first, second, amp):
    tile = lax.dot_general(first, second, (((0,), (0,)), ((), ())), preferred_element_type=jnp.float32)
    tile = tile.reshape(VB, VB, VB, VB).transpose(1, 3, 0, 2).reshape(VB * VB, VB * VB)
    tile = tile.astype(jnp.bfloat16)
    return jnp.dot(amp, tile, preferred_element_type=jnp.float32)


def task_term(first, second, amp):
    width = AUX // N_AUX
    total = jnp.zeros((amp.shape[0], VB * VB), jnp.float32)
    for quarter in range(N_AUX):
        lower = quarter * width
        total = total + quarter_term(first[lower:lower + width], second[lower:lower + width], amp)
    return total


def reference(factors, amplitudes, task_counts, task_tiles):
    owners = jnp.repeat(jnp.arange(TILES, dtype=jnp.int32), MOST)
    slots = jnp.tile(jnp.arange(MOST, dtype=jnp.int32), TILES)

    def step(total, item):
        owner, slot = item
        offs = task_tiles[owner, slot]
        idx = (owner + offs - RADIUS) % TILES
        live = slot < task_counts[owner]

        def compute(unused):
            return task_term(factors[idx[0]], factors[idx[1]], amplitudes[idx[2]])

        def empty(unused):
            return jnp.zeros((OCCP, VB * VB), jnp.float32)

        term = lax.cond(live, compute, empty, 0)
        total = lax.dynamic_update_index_in_dim(total, lax.dynamic_index_in_dim(total, owner, 0, False) + term, owner, 0)
        return total, 0

    start = jnp.zeros((TILES, OCCP, VB * VB), jnp.float32)
    total, unused = lax.scan(step, start, (owners, slots))
    return total
```

```python
import functools

import jax
import jax.numpy as jnp
from jax import lax
from jax.experimental import pallas as pl
from jax.experimental.pallas import tpu as pltpu
from jax.sharding import PartitionSpec as P

VB = 32
PAIRS = VB * VB
RADIUS = 2
SPAN = 2 * RADIUS + 1
FAR = 3
LANES = 128
GROUPS = LANES // VB
BF16 = jnp.bfloat16
F32 = jnp.float32
ANY = pl.BlockSpec(memory_space=pl.ANY)
SMEM = pl.BlockSpec(memory_space=pltpu.SMEM)
VMEM = pl.BlockSpec(memory_space=pltpu.VMEM)
NT = (((1,), (1,)), ((), ()))


def swap_matrix(dtype):
    row = lax.broadcasted_iota(jnp.int32, (PAIRS, PAIRS), 0)
    col = lax.broadcasted_iota(jnp.int32, (PAIRS, PAIRS), 1)
    hit = row == (col % VB) * VB + col // VB
    return jnp.where(hit, 1.0, 0.0).astype(dtype)


def own_kernel(fac, amp, flipped, amp_out, swap):
    swap[...] = swap_matrix(BF16)
    amp_out[...] = jnp.dot(amp[...], swap[...], preferred_element_type=F32).astype(BF16)
    flipped[...] = lax.dot_general(swap[...], fac[...], NT, preferred_element_type=F32).astype(BF16)


def flip_kernel(fac, flipped, swap):
    swap[...] = swap_matrix(BF16)
    flipped[...] = lax.dot_general(swap[...], fac[...], NT, preferred_element_type=F32).astype(BF16)


def prepare_own(fac, amp):
    quarter = fac.shape[0]
    return pl.pallas_call(
        own_kernel,
        out_shape=(
            jax.ShapeDtypeStruct((PAIRS, quarter), BF16),
            jax.ShapeDtypeStruct(amp.shape, BF16),
        ),
        in_specs=[VMEM, VMEM],
        out_specs=(VMEM, VMEM),
        scratch_shapes=[pltpu.VMEM((PAIRS, PAIRS), BF16)],
        compiler_params=pltpu.CompilerParams(vmem_limit_bytes=24 << 20),
        name="own",
    )(fac, amp)


def flip(fac):
    quarter = fac.shape[0]
    return pl.pallas_call(
        flip_kernel,
        out_shape=jax.ShapeDtypeStruct((PAIRS, quarter), BF16),
        in_specs=[VMEM],
        out_specs=VMEM,
        scratch_shapes=[pltpu.VMEM((PAIRS, PAIRS), BF16)],
        compiler_params=pltpu.CompilerParams(vmem_limit_bytes=24 << 20),
        name="flip",
    )(fac)


def roll_groups(x, groups):
    groups %= GROUPS
    return x if groups == 0 else pltpu.roll(x, groups * VB, 1)


def task_quarter(turned, fac_cols, amp, tile):
    product = jnp.dot(turned, fac_cols, preferred_element_type=F32)
    group = lax.broadcasted_iota(jnp.int32, (VB, LANES), 1) // VB
    for high in range(fac_cols.shape[1] // LANES):
        for d_high in range(VB // GROUPS):
            blocks = []
            for d_low in range(GROUPS):
                first = (d_high * GROUPS + d_low) * VB
                block = product[first : first + VB, high * LANES : (high + 1) * LANES]
                blocks.append(roll_groups(block, d_low))
            for a_low in range(GROUPS):
                mixed = blocks[(0 - a_low) % GROUPS]
                for j in range(1, GROUPS):
                    mixed = jnp.where(group == j, blocks[(j - a_low) % GROUPS], mixed)
                mixed = roll_groups(mixed, -a_low)
                first = (high * GROUPS + a_low) * VB
                tile[first : first + VB, d_high * LANES : (d_high + 1) * LANES] = mixed.astype(BF16)
    return lax.dot_general(amp, tile[...], NT, preferred_element_type=F32)


def start_one(index, sources, target, sem):
    for place, source in sources.items():

        @pl.when(index == place)
        def _():
            pltpu.make_async_copy(source, target, sem).start()


def tasks_kernel(count, plan, *refs, late, places):
    number = len(places)
    facs = dict(zip(places, refs[:number]))
    turned = dict(zip(places, refs[number : 2 * number]))
    amps = dict(enumerate(refs[2 * number : 2 * number + SPAN]))
    rest = refs[2 * number + SPAN :]
    if late:
        before, rest = rest[0], rest[1:]
    out, fac_buf, turn_buf, amp_buf, tile, sems = rest
    slots = plan.shape[0]
    columns = out.shape[2]

    def mine(slot):
        far = jnp.logical_or(plan[slot, 0] == FAR, plan[slot, 1] == FAR)
        return jnp.logical_and(slot < count[0], far if late else jnp.logical_not(far))

    for slot in range(slots):

        @pl.when(mine(slot))
        def _():
            start_one(plan[slot, 1], turned, turn_buf.at[slot], sems.at[slot, 0])
            start_one(plan[slot, 0], facs, fac_buf.at[slot], sems.at[slot, 1])
            start_one(plan[slot, 2], amps, amp_buf.at[slot], sems.at[slot, 2])

    if late:
        out[...] = before[...]
    else:
        out[...] = jnp.zeros_like(out)

    @pl.loop(0, slots)
    def _(slot):
        @pl.when(mine(slot))
        def _():
            pltpu.make_async_copy(turned[0], turn_buf.at[slot], sems.at[slot, 0]).wait()
            pltpu.make_async_copy(facs[0], fac_buf.at[slot], sems.at[slot, 1]).wait()
            pltpu.make_async_copy(amps[0], amp_buf.at[slot], sems.at[slot, 2]).wait()

            @pl.loop(0, out.shape[0])
            def _(part):
                cols = pl.ds(pl.multiple_of(part * columns, columns), columns)
                out[part] += task_quarter(
                    turn_buf[slot], fac_buf[slot, :, cols], amp_buf[slot], tile
                )


def run_tasks(count, plan, facs, turned, amps, before, parts):
    late = before is not None
    places = sorted(facs)
    quarter, occupied = facs[0].shape[0], amps[0].shape[0]
    slots = plan.shape[0]
    columns = PAIRS // parts
    operands = [facs[p] for p in places] + [turned[p] for p in places] + list(amps)
    specs = [ANY] * len(operands)
    if late:
        operands.append(before)
        specs.append(VMEM)
    return pl.pallas_call(
        functools.partial(tasks_kernel, late=late, places=places),
        out_shape=jax.ShapeDtypeStruct((parts, occupied, columns), F32),
        in_specs=[SMEM, SMEM] + specs,
        out_specs=VMEM,
        scratch_shapes=[
            pltpu.VMEM((slots, quarter, PAIRS), BF16),
            pltpu.VMEM((slots, PAIRS, quarter), BF16),
            pltpu.VMEM((slots, occupied, PAIRS), BF16),
            pltpu.VMEM((columns, PAIRS), BF16),
            pltpu.SemaphoreType.DMA((slots, 3)),
        ],
        compiler_params=pltpu.CompilerParams(vmem_limit_bytes=40 << 20),
        name="late" if late else "early",
    )(count, plan, *operands)


def shards(factors, amplitudes, task_counts, task_tiles):
    tiles = lax.axis_size("task")
    parts = lax.axis_size("aux")
    near = [((t + 2 if t % 2 == 0 else t - 2) % tiles, t) for t in range(tiles)]
    far = [((t - 2 if t % 2 == 0 else t + 2) % tiles, t) for t in range(tiles)]
    swap = [(t ^ 1, t) for t in range(tiles)]
    move = lambda x, route: lax.ppermute(x, "task", route)

    fac = factors[0]
    own_turned, own_amp = prepare_own(fac, amplitudes[0])
    sign = 1 - 2 * (lax.axis_index("task") % 2)
    plan = ((task_tiles[0] - RADIUS) * sign) % SPAN

    facs = {0: fac, 1: move(fac, swap), 2: move(fac, near), 3: move(fac, far)}
    facs[4] = move(facs[2], swap)
    amps = {0: own_amp, 1: move(own_amp, swap), 2: move(own_amp, near), 3: move(own_amp, far)}
    amps[4] = move(amps[2], swap)
    amps = [amps[p] for p in range(SPAN)]
    turned = {p: own_turned if p == 0 else flip(facs[p]) for p in range(SPAN)}
    without = lambda d: {p: d[p] for p in d if p != FAR}
    early = run_tasks(task_counts, plan, without(facs), without(turned), amps, None, parts)
    total = run_tasks(task_counts, plan, facs, turned, amps, early, parts)
    mine = lax.axis_index("aux")
    arrived = lax.all_to_all(total.astype(BF16), "aux", 0, 0, tiled=True).astype(F32)
    own = lax.dynamic_index_in_dim(total, mine, 0, False)
    keep = lax.broadcasted_iota(jnp.int32, (parts, 1, 1), 0) == mine
    return jnp.sum(jnp.where(keep, own[None], arrived), axis=0)[None]


def solution(mesh):
    return jax.shard_map(
        shards,
        mesh=mesh,
        in_specs=(P("task", "aux", None), P("task", None, None), P("task"), P("task", None, None)),
        out_specs=P("task", None, "aux"),
        check_vma=False,
    )
```

```python
import functools

import jax
import jax.numpy as jnp
from jax import lax
from jax.experimental import pallas as pl
from jax.experimental.pallas import tpu as pltpu
from jax.sharding import PartitionSpec as P

VB = 32
PAIRS = VB * VB
RADIUS = 2
SPAN = 2 * RADIUS + 1
FAR = 3
LANES = 128
GROUPS = LANES // VB
BF16 = jnp.bfloat16
F32 = jnp.float32
HBM = pl.BlockSpec(memory_space=pltpu.HBM)
SMEM = pl.BlockSpec(memory_space=pltpu.SMEM)
VMEM = pl.BlockSpec(memory_space=pltpu.VMEM)
NT = (((1,), (1,)), ((), ()))


def swap_matrix():
    row = lax.broadcasted_iota(jnp.int32, (PAIRS, PAIRS), 0)
    col = lax.broadcasted_iota(jnp.int32, (PAIRS, PAIRS), 1)
    hit = row == (col % VB) * VB + col // VB
    return jnp.where(hit, 1.0, 0.0).astype(BF16)


def params(mib):
    return pltpu.CompilerParams(vmem_limit_bytes=mib << 20)


def cost(flops, moved):
    return pl.CostEstimate(flops=flops, bytes_accessed=moved, transcendentals=0)


def pack_kernel(fac, amp, out, amp_out, swap, fac_buf, sems):
    depth = fac.shape[0]
    arrive = pltpu.make_async_copy(fac, fac_buf, sems.at[0])
    arrive.start()
    swap[...] = swap_matrix()
    arrive.wait()
    leave = pltpu.make_async_copy(fac_buf, out.at[:depth], sems.at[1])
    leave.start()
    amp_out[...] = jnp.dot(amp[...], swap[...], preferred_element_type=F32).astype(BF16)
    other = pltpu.make_async_copy(amp_out, out.at[depth:], sems.at[2])
    other.start()
    leave.wait()
    other.wait()


def pack(fac, amp):
    return pl.pallas_call(
        pack_kernel,
        out_shape=(
            jax.ShapeDtypeStruct((fac.shape[0] + amp.shape[0], PAIRS), BF16),
            jax.ShapeDtypeStruct(amp.shape, BF16),
        ),
        in_specs=[HBM, VMEM],
        out_specs=(HBM, VMEM),
        scratch_shapes=[
            pltpu.VMEM((PAIRS, PAIRS), BF16),
            pltpu.VMEM(fac.shape, BF16),
            pltpu.SemaphoreType.DMA((3,)),
        ],
        compiler_params=params(34),
        cost_estimate=cost(1, 1),
        name="pack",
    )(fac, amp)


def roll_groups(x, groups):
    groups %= GROUPS
    return x if groups == 0 else pltpu.roll(x, groups * VB, 1)


def write_tile(product, tile):
    group = lax.broadcasted_iota(jnp.int32, (VB, LANES), 1) // VB
    for high in range(PAIRS // LANES):
        for d_high in range(VB // GROUPS):
            blocks = []
            for d_low in range(GROUPS):
                first = (d_high * GROUPS + d_low) * VB
                block = product[first : first + VB, high * LANES : (high + 1) * LANES]
                blocks.append(roll_groups(block, d_low))
            for a_low in range(GROUPS):
                mixed = blocks[(0 - a_low) % GROUPS]
                for j in range(1, GROUPS):
                    mixed = jnp.where(group == j, blocks[(j - a_low) % GROUPS], mixed)
                first = high * LANES + a_low * VB
                tile[first : first + VB, d_high * LANES : (d_high + 1) * LANES] = roll_groups(
                    mixed, -a_low
                )


def start_one(index, sources, target, sem):
    for place, source in sources.items():

        @pl.when(index == place)
        def _():
            pltpu.make_async_copy(source, target, sem).start()


EMPTY, READY, FIRST, SECOND = range(4)


def slot_table(count, plan):
    sign = 1 - 2 * (lax.axis_index("task") % 2)
    distance = (plan - RADIUS) * sign
    places = jnp.where(distance < 0, distance + SPAN, distance)
    kind = jnp.where(places[:, 0] == FAR, FIRST, READY)
    kind = jnp.where(places[:, 1] == FAR, SECOND, kind)
    kind = jnp.where(jnp.arange(plan.shape[0]) < count[0], kind, EMPTY)
    return jnp.concatenate([kind[:, None], places], axis=1).astype(jnp.int32)


def any_slot(hits, slots):
    return functools.reduce(jnp.logical_or, [hits(slot) for slot in range(slots)])


def turn(swap, fac):
    return lax.dot_general(swap[...], fac, NT, preferred_element_type=F32).astype(BF16)


def early_kernel(table, own, partner, near, partner_near, out, turned_out, *scratch):
    left, right, turned, swap, tiles, sems = scratch
    depth, slots = near.shape[0], table.shape[0]
    facs = {0: own.at[:depth], 1: partner.at[:depth], 2: near, 4: partner_near}
    whole = lambda s: table[s, 0] == READY
    half = lambda s: table[s, 0] == FIRST
    mine = lambda s: jnp.logical_or(whole(s), half(s))
    tile_copy = lambda s: pltpu.make_async_copy(tiles.at[s], out.at[s], sems.at[s, 2])
    turned_copy = lambda s: pltpu.make_async_copy(turned.at[s], turned_out.at[s], sems.at[s, 3])
    for slot in range(slots):

        @pl.when(mine(slot))
        def _():
            start_one(table[slot, 2], facs, right.at[slot], sems.at[slot, 1])

        @pl.when(whole(slot))
        def _():
            start_one(table[slot, 1], facs, left.at[slot], sems.at[slot, 0])

    @pl.when(any_slot(mine, slots))
    def _():
        swap[...] = swap_matrix()

    @pl.loop(0, slots)
    def _(slot):
        @pl.when(mine(slot))
        def _():
            pltpu.make_async_copy(near, right.at[slot], sems.at[slot, 1]).wait()
            turned[slot] = turn(swap, right[slot])

        @pl.when(half(slot))
        def _():
            turned_copy(slot).start()

        @pl.when(whole(slot))
        def _():
            pltpu.make_async_copy(near, left.at[slot], sems.at[slot, 0]).wait()
            product = jnp.dot(turned[slot], left[slot], preferred_element_type=F32)
            write_tile(product.astype(BF16), tiles.at[slot])
            tile_copy(slot).start()

    for slot in range(slots):
        pl.when(whole(slot))(lambda: tile_copy(slot).wait())
        pl.when(half(slot))(lambda: turned_copy(slot).wait())


def turn_kernel(table, far, out, swap, fac, turned, sems):
    slots = table.shape[0]

    @pl.when(any_slot(lambda s: table[s, 0] == SECOND, slots))
    def _():
        arrive = pltpu.make_async_copy(far.at[: fac.shape[0]], fac, sems.at[0])
        arrive.start()
        swap[...] = swap_matrix()
        arrive.wait()
        turned[...] = turn(swap, fac[...])
        leave = pltpu.make_async_copy(turned, out, sems.at[1])
        leave.start()
        leave.wait()


def late_kernel(
    table, early, early_turned, far_turned, own, partner, near, partner_near, far, amp_2, amp_4, *refs
):
    sent, kept, total, amp_buf, left, turned, tiles, sems = refs
    depth, slots = near.shape[0], table.shape[0]
    facs = {0: own.at[:depth], 1: partner.at[:depth], 2: near, 3: far.at[:depth], 4: partner_near}
    amps = {0: own.at[depth:], 1: partner.at[depth:], 2: amp_2, 3: far.at[depth:], 4: amp_4}
    live = lambda s: table[s, 0] != EMPTY
    mine = lambda s: table[s, 0] >= FIRST
    made = lambda s: table[s, 0] == READY
    for slot in range(slots):

        @pl.when(mine(slot))
        def _():
            right_far = table[slot, 0] == SECOND

            @pl.when(right_far)
            def _():
                pltpu.make_async_copy(far_turned, turned.at[slot], sems.at[slot, 1]).start()

            @pl.when(jnp.logical_not(right_far))
            def _():
                pltpu.make_async_copy(early_turned.at[slot], turned.at[slot], sems.at[slot, 1]).start()

            start_one(table[slot, 1], facs, left.at[slot], sems.at[slot, 0])

        @pl.when(made(slot))
        def _():
            pltpu.make_async_copy(early.at[slot], tiles.at[slot], sems.at[slot, 2]).start()

        @pl.when(live(slot))
        def _():
            start_one(table[slot, 3], amps, amp_buf.at[slot], sems.at[slot, 3])

    total[...] = jnp.zeros_like(total)

    @pl.loop(0, slots)
    def _(slot):
        @pl.when(mine(slot))
        def _():
            pltpu.make_async_copy(far_turned, turned.at[slot], sems.at[slot, 1]).wait()
            pltpu.make_async_copy(near, left.at[slot], sems.at[slot, 0]).wait()
            product = jnp.dot(turned[slot], left[slot], preferred_element_type=F32)
            write_tile(product.astype(BF16), tiles.at[slot])

        @pl.when(made(slot))
        def _():
            pltpu.make_async_copy(early.at[slot], tiles.at[slot], sems.at[slot, 2]).wait()

        @pl.when(live(slot))
        def _():
            pltpu.make_async_copy(amp_2, amp_buf.at[slot], sems.at[slot, 3]).wait()
            total[...] += lax.dot_general(
                amp_buf[slot], tiles[slot], NT, preferred_element_type=F32
            )

    place = lax.axis_index("aux")
    columns = kept.shape[1]
    for part in range(sent.shape[0]):
        values = total[:, part * columns : (part + 1) * columns]
        sent[part] = jnp.where(place == part, 0.0, values).astype(BF16)
    kept[...] = total[:, pl.ds(pl.multiple_of(place * columns, columns), columns)]


def early_tiles(table, own, partner, near, partner_near):
    slots, quarter = table.shape[0], near.shape[0]
    return pl.pallas_call(
        early_kernel,
        out_shape=(
            jax.ShapeDtypeStruct((slots, PAIRS, PAIRS), BF16),
            jax.ShapeDtypeStruct((slots, PAIRS, quarter), BF16),
        ),
        in_specs=[SMEM] + [HBM] * 4,
        out_specs=(HBM, HBM),
        scratch_shapes=[
            pltpu.VMEM((slots, quarter, PAIRS), BF16),
            pltpu.VMEM((slots, quarter, PAIRS), BF16),
            pltpu.VMEM((slots, PAIRS, quarter), BF16),
            pltpu.VMEM((PAIRS, PAIRS), BF16),
            pltpu.VMEM((slots, PAIRS, PAIRS), BF16),
            pltpu.SemaphoreType.DMA((slots, 4)),
        ],
        compiler_params=params(34),
        cost_estimate=cost(1, 1),
        name="early",
    )(table, own, partner, near, partner_near)


def turn_far(table, far, quarter):
    return pl.pallas_call(
        turn_kernel,
        out_shape=jax.ShapeDtypeStruct((PAIRS, quarter), BF16),
        in_specs=[SMEM, HBM],
        out_specs=HBM,
        scratch_shapes=[
            pltpu.VMEM((PAIRS, PAIRS), BF16),
            pltpu.VMEM((quarter, PAIRS), BF16),
            pltpu.VMEM((PAIRS, quarter), BF16),
            pltpu.SemaphoreType.DMA((2,)),
        ],
        compiler_params=params(34),
        cost_estimate=cost(20 * quarter * PAIRS * PAIRS, 1 << 20),
        name="turn",
    )(table, far)


def all_terms(table, early, early_turned, far_turned, own, partner, near, partner_near, far, amp_2, amp_4, parts):
    slots, columns, occupied, quarter = table.shape[0], PAIRS // parts, amp_2.shape[0], near.shape[0]
    return pl.pallas_call(
        late_kernel,
        out_shape=(
            jax.ShapeDtypeStruct((parts, occupied, columns), BF16),
            jax.ShapeDtypeStruct((occupied, columns), F32),
        ),
        in_specs=[SMEM] + [HBM] * 10,
        out_specs=(VMEM, VMEM),
        scratch_shapes=[
            pltpu.VMEM((occupied, PAIRS), F32),
            pltpu.VMEM((slots, occupied, PAIRS), BF16),
            pltpu.VMEM((slots, quarter, PAIRS), BF16),
            pltpu.VMEM((slots, PAIRS, quarter), BF16),
            pltpu.VMEM((slots, PAIRS, PAIRS), BF16),
            pltpu.SemaphoreType.DMA((slots, 4)),
        ],
        compiler_params=params(34),
        cost_estimate=cost(1, 1),
        name="late",
    )(table, early, early_turned, far_turned, own, partner, near, partner_near, far, amp_2, amp_4)


def after(x, *others):
    return lax.optimization_barrier((x, *others))[0]


def shards(factors, amplitudes, task_counts, task_tiles):
    tiles = lax.axis_size("task")
    parts = lax.axis_size("aux")
    near = [((t + 2 if t % 2 == 0 else t - 2) % tiles, t) for t in range(tiles)]
    far = [((t - 2 if t % 2 == 0 else t + 2) % tiles, t) for t in range(tiles)]
    swap = [(t ^ 1, t) for t in range(tiles)]
    move = lambda x, route: lax.ppermute(x, "task", route)

    fac = factors[0]
    table = slot_table(task_counts, task_tiles[0])
    fac_2 = move(fac, near)
    own, amp = pack(fac, amplitudes[0])
    packed_3 = move(own, far)
    packed_1 = move(own, swap)
    amp_2 = move(amp, near)
    fac_4 = move(fac_2, swap)
    early, early_turned = early_tiles(table, own, packed_1, fac_2, fac_4)
    amp_4 = move(after(amp_2, early), swap)
    far_turned = turn_far(table, packed_3, fac.shape[0])
    sent, kept = all_terms(
        table,
        early,
        early_turned,
        far_turned,
        own,
        packed_1,
        fac_2,
        fac_4,
        packed_3,
        amp_2,
        amp_4,
        parts,
    )
    arrived = lax.all_to_all(sent, "aux", 0, 0, tiled=True)
    return (kept + jnp.sum(arrived.astype(F32), axis=0))[None]


def solution(mesh):
    return jax.shard_map(
        shards,
        mesh=mesh,
        in_specs=(P("task", "aux", None), P("task", None, None), P("task"), P("task", None, None)),
        out_specs=P("task", None, "aux"),
        check_vma=False,
    )
```

```python
import functools

import jax
import jax.numpy as jnp
from jax import lax
from jax.experimental import pallas as pl
from jax.experimental.pallas import tpu as pltpu
from jax.sharding import PartitionSpec as P

VB = 32
PAIRS = VB * VB
RADIUS = 2
SPAN = 2 * RADIUS + 1
FAR = 3
LANES = 128
GROUPS = LANES // VB
BF16 = jnp.bfloat16
F32 = jnp.float32
HBM = pl.BlockSpec(memory_space=pltpu.HBM)
SMEM = pl.BlockSpec(memory_space=pltpu.SMEM)
VMEM = pl.BlockSpec(memory_space=pltpu.VMEM)
NT = (((1,), (1,)), ((), ()))


def swap_matrix():
    row = lax.broadcasted_iota(jnp.int32, (PAIRS, PAIRS), 0)
    col = lax.broadcasted_iota(jnp.int32, (PAIRS, PAIRS), 1)
    hit = row == (col % VB) * VB + col // VB
    return jnp.where(hit, 1.0, 0.0).astype(BF16)


def params(mib):
    return pltpu.CompilerParams(vmem_limit_bytes=mib << 20)


def cost(flops, moved):
    return pl.CostEstimate(flops=flops, bytes_accessed=moved, transcendentals=0)


def amp_kernel(amp, out, swap):
    swap[...] = swap_matrix()
    out[...] = jnp.dot(amp[...], swap[...], preferred_element_type=F32).astype(BF16)


def swapped_pairs(amp):
    return pl.pallas_call(
        amp_kernel,
        out_shape=jax.ShapeDtypeStruct(amp.shape, BF16),
        in_specs=[VMEM],
        out_specs=VMEM,
        scratch_shapes=[pltpu.VMEM((PAIRS, PAIRS), BF16)],
        compiler_params=params(16),
        cost_estimate=cost(1, 1),
        name="amp",
    )(amp)


def pack_kernel(fac, amp, out, amp_out, swap, fac_buf, sems):
    depth = fac.shape[0]
    arrive = pltpu.make_async_copy(fac, fac_buf, sems.at[0])
    arrive.start()
    swap[...] = swap_matrix()
    arrive.wait()
    leave = pltpu.make_async_copy(fac_buf, out.at[:depth], sems.at[1])
    leave.start()
    amp_out[...] = jnp.dot(amp[...], swap[...], preferred_element_type=F32).astype(BF16)
    other = pltpu.make_async_copy(amp_out, out.at[depth:], sems.at[2])
    other.start()
    leave.wait()
    other.wait()


def pack(fac, amp):
    return pl.pallas_call(
        pack_kernel,
        out_shape=(
            jax.ShapeDtypeStruct((fac.shape[0] + amp.shape[0], PAIRS), BF16),
            jax.ShapeDtypeStruct(amp.shape, BF16),
        ),
        in_specs=[HBM, VMEM],
        out_specs=(HBM, VMEM),
        scratch_shapes=[
            pltpu.VMEM((PAIRS, PAIRS), BF16),
            pltpu.VMEM(fac.shape, BF16),
            pltpu.SemaphoreType.DMA((3,)),
        ],
        compiler_params=params(34),
        cost_estimate=cost(1, 1),
        name="pack",
    )(fac, amp)


def roll_groups(x, groups):
    groups %= GROUPS
    return x if groups == 0 else pltpu.roll(x, groups * VB, 1)


def write_tile(product, tile):
    group = lax.broadcasted_iota(jnp.int32, (VB, LANES), 1) // VB
    for high in range(PAIRS // LANES):
        for d_high in range(VB // GROUPS):
            blocks = []
            for d_low in range(GROUPS):
                first = (d_high * GROUPS + d_low) * VB
                block = product[first : first + VB, high * LANES : (high + 1) * LANES]
                blocks.append(roll_groups(block, d_low))
            for a_low in range(GROUPS):
                mixed = blocks[(0 - a_low) % GROUPS]
                for j in range(1, GROUPS):
                    mixed = jnp.where(group == j, blocks[(j - a_low) % GROUPS], mixed)
                first = high * LANES + a_low * VB
                tile[first : first + VB, d_high * LANES : (d_high + 1) * LANES] = roll_groups(
                    mixed, -a_low
                )


def start_one(index, sources, target, sem):
    for place, source in sources.items():

        @pl.when(index == place)
        def _():
            pltpu.make_async_copy(source, target, sem).start()


EMPTY, READY, FIRST, SECOND = range(4)


def slot_table(count, plan):
    sign = 1 - 2 * (lax.axis_index("task") % 2)
    distance = (plan - RADIUS) * sign
    places = jnp.where(distance < 0, distance + SPAN, distance)
    kind = jnp.where(places[:, 0] == FAR, FIRST, READY)
    kind = jnp.where(places[:, 1] == FAR, SECOND, kind)
    kind = jnp.where(jnp.arange(plan.shape[0]) < count[0], kind, EMPTY)
    return jnp.concatenate([kind[:, None], places], axis=1).astype(jnp.int32)


def any_slot(hits, slots):
    return functools.reduce(jnp.logical_or, [hits(slot) for slot in range(slots)])


def turn(swap, fac):
    return lax.dot_general(swap[...], fac, NT, preferred_element_type=F32).astype(BF16)


def early_kernel(table, own, partner, near, partner_near, out, turned_out, *scratch):
    left, right, turned, swap, tiles, sems = scratch
    depth, slots = near.shape[0], table.shape[0]
    facs = {0: own.at[:depth], 1: partner.at[:depth], 2: near, 4: partner_near}
    whole = lambda s: table[s, 0] == READY
    half = lambda s: table[s, 0] == FIRST
    mine = lambda s: jnp.logical_or(whole(s), half(s))
    tile_copy = lambda s: pltpu.make_async_copy(tiles.at[s], out.at[s], sems.at[s, 2])
    turned_copy = lambda s: pltpu.make_async_copy(turned.at[s], turned_out.at[s], sems.at[s, 3])
    for slot in range(slots):

        @pl.when(mine(slot))
        def _():
            start_one(table[slot, 2], facs, right.at[slot], sems.at[slot, 1])

        @pl.when(whole(slot))
        def _():
            start_one(table[slot, 1], facs, left.at[slot], sems.at[slot, 0])

    @pl.when(any_slot(mine, slots))
    def _():
        swap[...] = swap_matrix()

    @pl.loop(0, slots)
    def _(slot):
        @pl.when(mine(slot))
        def _():
            pltpu.make_async_copy(near, right.at[slot], sems.at[slot, 1]).wait()
            turned[slot] = turn(swap, right[slot])

        @pl.when(half(slot))
        def _():
            turned_copy(slot).start()

        @pl.when(whole(slot))
        def _():
            pltpu.make_async_copy(near, left.at[slot], sems.at[slot, 0]).wait()
            product = jnp.dot(turned[slot], left[slot], preferred_element_type=F32)
            write_tile(product.astype(BF16), tiles.at[slot])
            tile_copy(slot).start()

    for slot in range(slots):
        pl.when(whole(slot))(lambda: tile_copy(slot).wait())
        pl.when(half(slot))(lambda: turned_copy(slot).wait())


def turn_kernel(table, far, out, swap, fac, turned, sems):
    slots = table.shape[0]

    @pl.when(any_slot(lambda s: table[s, 0] == SECOND, slots))
    def _():
        arrive = pltpu.make_async_copy(far.at[: fac.shape[0]], fac, sems.at[0])
        arrive.start()
        swap[...] = swap_matrix()
        arrive.wait()
        turned[...] = turn(swap, fac[...])
        leave = pltpu.make_async_copy(turned, out, sems.at[1])
        leave.start()
        leave.wait()


def late_kernel(
    table, early, early_turned, far_turned, own, partner, near, partner_near, far, amp_2, amp_4, *refs
):
    sent, kept, total, amp_buf, left, turned, tiles, sems = refs
    depth, slots = near.shape[0], table.shape[0]
    facs = {0: own.at[:depth], 1: partner.at[:depth], 2: near, 3: far.at[:depth], 4: partner_near}
    amps = {0: own.at[depth:], 1: partner.at[depth:], 2: amp_2, 3: far.at[depth:], 4: amp_4}
    live = lambda s: table[s, 0] != EMPTY
    mine = lambda s: table[s, 0] >= FIRST
    made = lambda s: table[s, 0] == READY
    for slot in range(slots):

        @pl.when(mine(slot))
        def _():
            right_far = table[slot, 0] == SECOND

            @pl.when(right_far)
            def _():
                pltpu.make_async_copy(far_turned, turned.at[slot], sems.at[slot, 1]).start()

            @pl.when(jnp.logical_not(right_far))
            def _():
                pltpu.make_async_copy(early_turned.at[slot], turned.at[slot], sems.at[slot, 1]).start()

            start_one(table[slot, 1], facs, left.at[slot], sems.at[slot, 0])

        @pl.when(made(slot))
        def _():
            pltpu.make_async_copy(early.at[slot], tiles.at[slot], sems.at[slot, 2]).start()

        @pl.when(live(slot))
        def _():
            start_one(table[slot, 3], amps, amp_buf.at[slot], sems.at[slot, 3])

    total[...] = jnp.zeros_like(total)

    @pl.loop(0, slots)
    def _(slot):
        @pl.when(mine(slot))
        def _():
            pltpu.make_async_copy(far_turned, turned.at[slot], sems.at[slot, 1]).wait()
            pltpu.make_async_copy(near, left.at[slot], sems.at[slot, 0]).wait()
            product = jnp.dot(turned[slot], left[slot], preferred_element_type=F32)
            write_tile(product.astype(BF16), tiles.at[slot])

        @pl.when(made(slot))
        def _():
            pltpu.make_async_copy(early.at[slot], tiles.at[slot], sems.at[slot, 2]).wait()

        @pl.when(live(slot))
        def _():
            pltpu.make_async_copy(amp_2, amp_buf.at[slot], sems.at[slot, 3]).wait()
            total[...] += lax.dot_general(
                amp_buf[slot], tiles[slot], NT, preferred_element_type=F32
            )

    place = lax.axis_index("aux")
    columns = kept.shape[1]
    for part in range(sent.shape[0]):
        values = total[:, part * columns : (part + 1) * columns]
        sent[part] = jnp.where(place == part, 0.0, values).astype(BF16)
    kept[...] = total[:, pl.ds(pl.multiple_of(place * columns, columns), columns)]


def early_tiles(table, own, partner, near, partner_near):
    slots, quarter = table.shape[0], near.shape[0]
    return pl.pallas_call(
        early_kernel,
        out_shape=(
            jax.ShapeDtypeStruct((slots, PAIRS, PAIRS), BF16),
            jax.ShapeDtypeStruct((slots, PAIRS, quarter), BF16),
        ),
        in_specs=[SMEM] + [HBM] * 4,
        out_specs=(HBM, HBM),
        scratch_shapes=[
            pltpu.VMEM((slots, quarter, PAIRS), BF16),
            pltpu.VMEM((slots, quarter, PAIRS), BF16),
            pltpu.VMEM((slots, PAIRS, quarter), BF16),
            pltpu.VMEM((PAIRS, PAIRS), BF16),
            pltpu.VMEM((slots, PAIRS, PAIRS), BF16),
            pltpu.SemaphoreType.DMA((slots, 4)),
        ],
        compiler_params=params(34),
        cost_estimate=cost(1, 1),
        name="early",
    )(table, own, partner, near, partner_near)


def turn_far(table, far, quarter):
    return pl.pallas_call(
        turn_kernel,
        out_shape=jax.ShapeDtypeStruct((PAIRS, quarter), BF16),
        in_specs=[SMEM, HBM],
        out_specs=HBM,
        scratch_shapes=[
            pltpu.VMEM((PAIRS, PAIRS), BF16),
            pltpu.VMEM((quarter, PAIRS), BF16),
            pltpu.VMEM((PAIRS, quarter), BF16),
            pltpu.SemaphoreType.DMA((2,)),
        ],
        compiler_params=params(34),
        cost_estimate=cost(20 * quarter * PAIRS * PAIRS, 1 << 20),
        name="turn",
    )(table, far)


def all_terms(table, early, early_turned, far_turned, own, partner, near, partner_near, far, amp_2, amp_4, parts):
    slots, columns, occupied, quarter = table.shape[0], PAIRS // parts, amp_2.shape[0], near.shape[0]
    return pl.pallas_call(
        late_kernel,
        out_shape=(
            jax.ShapeDtypeStruct((parts, occupied, columns), BF16),
            jax.ShapeDtypeStruct((occupied, columns), F32),
        ),
        in_specs=[SMEM] + [HBM] * 10,
        out_specs=(VMEM, VMEM),
        scratch_shapes=[
            pltpu.VMEM((occupied, PAIRS), F32),
            pltpu.VMEM((slots, occupied, PAIRS), BF16),
            pltpu.VMEM((slots, quarter, PAIRS), BF16),
            pltpu.VMEM((slots, PAIRS, quarter), BF16),
            pltpu.VMEM((slots, PAIRS, PAIRS), BF16),
            pltpu.SemaphoreType.DMA((slots, 4)),
        ],
        compiler_params=params(34),
        cost_estimate=cost(1, 1),
        name="late",
    )(table, early, early_turned, far_turned, own, partner, near, partner_near, far, amp_2, amp_4)


def after(x, *others):
    return lax.optimization_barrier((x, *others))[0]


def shards(factors, amplitudes, task_counts, task_tiles):
    tiles = lax.axis_size("task")
    parts = lax.axis_size("aux")
    near = [((t + 2 if t % 2 == 0 else t - 2) % tiles, t) for t in range(tiles)]
    far = [((t - 2 if t % 2 == 0 else t + 2) % tiles, t) for t in range(tiles)]
    swap = [(t ^ 1, t) for t in range(tiles)]
    move = lambda x, route: lax.ppermute(x, "task", route)

    fac = factors[0]
    table = slot_table(task_counts, task_tiles[0])
    fac_2 = move(fac, near)
    own, _ = pack(fac, amplitudes[0])
    packed_3 = move(own, far)
    packed_1 = move(own, swap)
    amp_2 = swapped_pairs(move(amplitudes[0], near))
    fac_4 = move(after(fac_2, amp_2), swap)
    amp_4 = move(amp_2, swap)
    early, early_turned = early_tiles(after(table, amp_4), own, packed_1, fac_2, fac_4)
    far_turned = turn_far(after(table, early), packed_3, fac.shape[0])
    sent, kept = all_terms(
        table,
        early,
        early_turned,
        far_turned,
        own,
        packed_1,
        fac_2,
        fac_4,
        packed_3,
        amp_2,
        amp_4,
        parts,
    )
    arrived = lax.all_to_all(sent, "aux", 0, 0, tiled=True)
    return (kept + jnp.sum(arrived.astype(F32), axis=0))[None]


def solution(mesh):
    return jax.shard_map(
        shards,
        mesh=mesh,
        in_specs=(P("task", "aux", None), P("task", None, None), P("task"), P("task", None, None)),
        out_specs=P("task", None, "aux"),
        check_vma=False,
    )
```

```python
import functools

import jax
import jax.numpy as jnp
from jax import lax
from jax.experimental import pallas as pl
from jax.experimental.pallas import tpu as pltpu
from jax.sharding import PartitionSpec as P

VB = 32
PAIRS = VB * VB
RADIUS = 2
SPAN = 2 * RADIUS + 1
FAR = 3
LANES = 128
GROUPS = LANES // VB
BF16 = jnp.bfloat16
F32 = jnp.float32
HBM = pl.BlockSpec(memory_space=pltpu.HBM)
SMEM = pl.BlockSpec(memory_space=pltpu.SMEM)
VMEM = pl.BlockSpec(memory_space=pltpu.VMEM)
NT = (((1,), (1,)), ((), ()))


def swap_matrix():
    row = lax.broadcasted_iota(jnp.int32, (PAIRS, PAIRS), 0)
    col = lax.broadcasted_iota(jnp.int32, (PAIRS, PAIRS), 1)
    hit = row == (col % VB) * VB + col // VB
    return jnp.where(hit, 1.0, 0.0).astype(BF16)


def params(mib):
    return pltpu.CompilerParams(vmem_limit_bytes=mib << 20)


def cost(flops, moved):
    return pl.CostEstimate(flops=flops, bytes_accessed=moved, transcendentals=0)


def amp_kernel(amp, out, swap):
    swap[...] = swap_matrix()
    out[...] = jnp.dot(amp[...], swap[...], preferred_element_type=F32).astype(BF16)


def swapped_pairs(amp):
    return pl.pallas_call(
        amp_kernel,
        out_shape=jax.ShapeDtypeStruct(amp.shape, BF16),
        in_specs=[VMEM],
        out_specs=VMEM,
        scratch_shapes=[pltpu.VMEM((PAIRS, PAIRS), BF16)],
        compiler_params=params(16),
        cost_estimate=cost(1, 1),
        name="amp",
    )(amp)


def pack_kernel(fac, amp, out, amp_out, swap, fac_buf, sems):
    depth = fac.shape[0]
    arrive = pltpu.make_async_copy(fac, fac_buf, sems.at[0])
    arrive.start()
    swap[...] = swap_matrix()
    arrive.wait()
    leave = pltpu.make_async_copy(fac_buf, out.at[:depth], sems.at[1])
    leave.start()
    amp_out[...] = jnp.dot(amp[...], swap[...], preferred_element_type=F32).astype(BF16)
    other = pltpu.make_async_copy(amp_out, out.at[depth:], sems.at[2])
    other.start()
    leave.wait()
    other.wait()


def pack(fac, amp):
    return pl.pallas_call(
        pack_kernel,
        out_shape=(
            jax.ShapeDtypeStruct((fac.shape[0] + amp.shape[0], PAIRS), BF16),
            jax.ShapeDtypeStruct(amp.shape, BF16),
        ),
        in_specs=[HBM, VMEM],
        out_specs=(HBM, VMEM),
        scratch_shapes=[
            pltpu.VMEM((PAIRS, PAIRS), BF16),
            pltpu.VMEM(fac.shape, BF16),
            pltpu.SemaphoreType.DMA((3,)),
        ],
        compiler_params=params(34),
        cost_estimate=cost(1, 1),
        name="pack",
    )(fac, amp)


def roll_groups(x, groups):
    groups %= GROUPS
    return x if groups == 0 else pltpu.roll(x, groups * VB, 1)


def write_tile(product, tile):
    group = lax.broadcasted_iota(jnp.int32, (VB, LANES), 1) // VB
    for high in range(PAIRS // LANES):
        for d_high in range(VB // GROUPS):
            blocks = []
            for d_low in range(GROUPS):
                first = (d_high * GROUPS + d_low) * VB
                block = product[first : first + VB, high * LANES : (high + 1) * LANES]
                blocks.append(roll_groups(block, d_low))
            for a_low in range(GROUPS):
                mixed = blocks[(0 - a_low) % GROUPS]
                for j in range(1, GROUPS):
                    mixed = jnp.where(group == j, blocks[(j - a_low) % GROUPS], mixed)
                first = high * LANES + a_low * VB
                tile[first : first + VB, d_high * LANES : (d_high + 1) * LANES] = roll_groups(
                    mixed, -a_low
                )


def start_one(index, sources, target, sem):
    for place, source in sources.items():

        @pl.when(index == place)
        def _():
            pltpu.make_async_copy(source, target, sem).start()


EMPTY, READY, FIRST, SECOND = range(4)


def slot_table(count, plan):
    sign = 1 - 2 * (lax.axis_index("task") % 2)
    distance = (plan - RADIUS) * sign
    places = jnp.where(distance < 0, distance + SPAN, distance)
    kind = jnp.where(places[:, 0] == FAR, FIRST, READY)
    kind = jnp.where(places[:, 1] == FAR, SECOND, kind)
    kind = jnp.where(jnp.arange(plan.shape[0]) < count[0], kind, EMPTY)
    return jnp.concatenate([kind[:, None], places], axis=1).astype(jnp.int32)


def any_slot(hits, slots):
    return functools.reduce(jnp.logical_or, [hits(slot) for slot in range(slots)])


def turn(swap, fac):
    return lax.dot_general(swap[...], fac, NT, preferred_element_type=F32).astype(BF16)


def early_kernel(table, own, partner, near, partner_near, out, turned_out, *scratch):
    left, right, turned, swap, tiles, sems = scratch
    depth, slots = near.shape[0], table.shape[0]
    facs = {0: own.at[:depth], 1: partner.at[:depth], 2: near, 4: partner_near}
    whole = lambda s: table[s, 0] == READY
    half = lambda s: table[s, 0] == FIRST
    mine = lambda s: jnp.logical_or(whole(s), half(s))
    tile_copy = lambda s: pltpu.make_async_copy(tiles.at[s], out.at[s], sems.at[s, 2])
    turned_copy = lambda s: pltpu.make_async_copy(turned.at[s], turned_out.at[s], sems.at[s, 3])
    for slot in range(slots):

        @pl.when(mine(slot))
        def _():
            start_one(table[slot, 2], facs, right.at[slot], sems.at[slot, 1])

        @pl.when(whole(slot))
        def _():
            start_one(table[slot, 1], facs, left.at[slot], sems.at[slot, 0])

    @pl.when(any_slot(mine, slots))
    def _():
        swap[...] = swap_matrix()

    @pl.loop(0, slots)
    def _(slot):
        @pl.when(mine(slot))
        def _():
            pltpu.make_async_copy(near, right.at[slot], sems.at[slot, 1]).wait()
            turned[slot] = turn(swap, right[slot])

        @pl.when(half(slot))
        def _():
            turned_copy(slot).start()

        @pl.when(whole(slot))
        def _():
            pltpu.make_async_copy(near, left.at[slot], sems.at[slot, 0]).wait()
            product = jnp.dot(turned[slot], left[slot], preferred_element_type=F32)
            write_tile(product.astype(BF16), tiles.at[slot])
            tile_copy(slot).start()

    for slot in range(slots):
        pl.when(whole(slot))(lambda: tile_copy(slot).wait())
        pl.when(half(slot))(lambda: turned_copy(slot).wait())


def late_kernel(
    table, early, early_turned, own, partner, near, partner_near, far, amp_2, amp_4, *refs
):
    sent, kept, total, amp_buf, left, right, turned, swap, tiles, sems, far_sem = refs
    depth, slots = near.shape[0], table.shape[0]
    facs = {0: own.at[:depth], 1: partner.at[:depth], 2: near, 3: far.at[:depth], 4: partner_near}
    amps = {0: own.at[depth:], 1: partner.at[depth:], 2: amp_2, 3: far.at[depth:], 4: amp_4}
    live = lambda s: table[s, 0] != EMPTY
    mine = lambda s: table[s, 0] >= FIRST
    made = lambda s: table[s, 0] == READY
    some = any_slot(lambda s: table[s, 0] == SECOND, slots)
    far_copy = pltpu.make_async_copy(facs[FAR], right, far_sem.at[0])
    turned_copy = lambda s: pltpu.make_async_copy(early_turned.at[s], turned.at[s], sems.at[s, 1])
    pl.when(some)(lambda: far_copy.start())
    for slot in range(slots):
        pl.when(table[slot, 0] == FIRST)(lambda: turned_copy(slot).start())

        @pl.when(mine(slot))
        def _():
            start_one(table[slot, 1], facs, left.at[slot], sems.at[slot, 0])

        @pl.when(made(slot))
        def _():
            pltpu.make_async_copy(early.at[slot], tiles.at[slot], sems.at[slot, 2]).start()

        @pl.when(live(slot))
        def _():
            start_one(table[slot, 3], amps, amp_buf.at[slot], sems.at[slot, 3])

    total[...] = jnp.zeros_like(total)

    @pl.when(some)
    def _():
        swap[...] = swap_matrix()
        far_copy.wait()
        turned[slots] = turn(swap, right[...])

    @pl.loop(0, slots)
    def _(slot):
        pl.when(table[slot, 0] == FIRST)(lambda: turned_copy(slot).wait())

        @pl.when(mine(slot))
        def _():
            pltpu.make_async_copy(near, left.at[slot], sems.at[slot, 0]).wait()
            place = jnp.where(table[slot, 0] == SECOND, slots, slot)
            product = jnp.dot(turned[place], left[slot], preferred_element_type=F32)
            write_tile(product.astype(BF16), tiles.at[slot])

        @pl.when(made(slot))
        def _():
            pltpu.make_async_copy(early.at[slot], tiles.at[slot], sems.at[slot, 2]).wait()

        @pl.when(live(slot))
        def _():
            pltpu.make_async_copy(amp_2, amp_buf.at[slot], sems.at[slot, 3]).wait()
            total[...] += lax.dot_general(
                amp_buf[slot], tiles[slot], NT, preferred_element_type=F32
            )

    place = lax.axis_index("aux")
    columns = kept.shape[1]
    for part in range(sent.shape[0]):
        values = total[:, part * columns : (part + 1) * columns]
        sent[part] = jnp.where(place == part, 0.0, values).astype(BF16)
    kept[...] = total[:, pl.ds(pl.multiple_of(place * columns, columns), columns)]


def early_tiles(table, own, partner, near, partner_near):
    slots, quarter = table.shape[0], near.shape[0]
    return pl.pallas_call(
        early_kernel,
        out_shape=(
            jax.ShapeDtypeStruct((slots, PAIRS, PAIRS), BF16),
            jax.ShapeDtypeStruct((slots, PAIRS, quarter), BF16),
        ),
        in_specs=[SMEM] + [HBM] * 4,
        out_specs=(HBM, HBM),
        scratch_shapes=[
            pltpu.VMEM((slots, quarter, PAIRS), BF16),
            pltpu.VMEM((slots, quarter, PAIRS), BF16),
            pltpu.VMEM((slots, PAIRS, quarter), BF16),
            pltpu.VMEM((PAIRS, PAIRS), BF16),
            pltpu.VMEM((slots, PAIRS, PAIRS), BF16),
            pltpu.SemaphoreType.DMA((slots, 4)),
        ],
        compiler_params=params(34),
        cost_estimate=cost(1, 1),
        name="early",
    )(table, own, partner, near, partner_near)


def all_terms(table, early, early_turned, own, partner, near, partner_near, far, amp_2, amp_4, parts):
    slots, columns, occupied, quarter = table.shape[0], PAIRS // parts, amp_2.shape[0], near.shape[0]
    return pl.pallas_call(
        late_kernel,
        out_shape=(
            jax.ShapeDtypeStruct((parts, occupied, columns), BF16),
            jax.ShapeDtypeStruct((occupied, columns), F32),
        ),
        in_specs=[SMEM] + [HBM] * 9,
        out_specs=(VMEM, VMEM),
        scratch_shapes=[
            pltpu.VMEM((occupied, PAIRS), F32),
            pltpu.VMEM((slots, occupied, PAIRS), BF16),
            pltpu.VMEM((slots, quarter, PAIRS), BF16),
            pltpu.VMEM((quarter, PAIRS), BF16),
            pltpu.VMEM((slots + 1, PAIRS, quarter), BF16),
            pltpu.VMEM((PAIRS, PAIRS), BF16),
            pltpu.VMEM((slots, PAIRS, PAIRS), BF16),
            pltpu.SemaphoreType.DMA((slots, 4)),
            pltpu.SemaphoreType.DMA((1,)),
        ],
        compiler_params=params(29),
        cost_estimate=cost(1, 1),
        name="late",
    )(table, early, early_turned, own, partner, near, partner_near, far, amp_2, amp_4)


def after(x, *others):
    return lax.optimization_barrier((x, *others))[0]


def shards(factors, amplitudes, task_counts, task_tiles):
    tiles = lax.axis_size("task")
    parts = lax.axis_size("aux")
    near = [((t + 2 if t % 2 == 0 else t - 2) % tiles, t) for t in range(tiles)]
    far = [((t - 2 if t % 2 == 0 else t + 2) % tiles, t) for t in range(tiles)]
    swap = [(t ^ 1, t) for t in range(tiles)]
    move = lambda x, route: lax.ppermute(x, "task", route)

    fac = factors[0]
    table = slot_table(task_counts, task_tiles[0])
    fac_2 = move(fac, near)
    own, _ = pack(fac, amplitudes[0])
    packed_3 = move(own, far)
    packed_1 = move(own, swap)
    amp_2 = swapped_pairs(move(amplitudes[0], near))
    fac_4 = move(after(fac_2, amp_2), swap)
    amp_4 = move(amp_2, swap)
    early, early_turned = early_tiles(after(table, amp_4), own, packed_1, fac_2, fac_4)
    sent, kept = all_terms(
        table,
        early,
        early_turned,
        own,
        packed_1,
        fac_2,
        fac_4,
        packed_3,
        amp_2,
        amp_4,
        parts,
    )
    arrived = lax.all_to_all(sent, "aux", 0, 0, tiled=True)
    return (kept + jnp.sum(arrived.astype(F32), axis=0))[None]


def solution(mesh):
    return jax.shard_map(
        shards,
        mesh=mesh,
        in_specs=(P("task", "aux", None), P("task", None, None), P("task"), P("task", None, None)),
        out_specs=P("task", None, "aux"),
        check_vma=False,
    )
```
